32 devices in a mesh: section: 4 (over y, x), lon: 8 (over z, core).
Axes of the slice: x: 2, y: 2, z: 4, core: 2. Of those that a mesh axis runs over, the one named last changes fastest.
Arguments:
- section_inputs: bfloat16 [4, 2, 32, 64, 256], P('section', None, None, 'lon'), may hold values from -6 to 6
- weights: bfloat16 [4, 2, 3, 3, 256, 256], P('section'), may hold values from -0.125 to 0.125
- out_cot: bfloat16 [2, 32, 64, 256], P(None, None, 'lon'), may hold values from -6 to 6
Outputs:
- act_grads: bfloat16 [4, 2, 32, 64, 256], P('section', None, None, 'lon')
- weight_grads: float32 [4, 2, 3, 3, 256, 256], P('section')
The draws below stay inside these ranges and needn't reach their ends.
All inputs are finite; a program needn't handle non-finite values.
Results may differ from the reference program's by a relative error of at most 0.02.
Values may be sent and summed in bfloat16 or wider, within the bound.
A program may use at most 64 MiB of HBM per device.

```python
import math
import jax
import jax.numpy as jnp
from jax import lax

C = 256
LAT = 32
MICRO = 2
NLON = 64
SECTIONS = 4


def block_scale(rng, shape, pieces, low, high):
    gain = 1.0
    for axis_at, blocks in pieces:
        heights = jax.random.uniform(jax.random.fold_in(jax.random.fold_in(rng, 6), axis_at), (blocks,), jnp.float32, low / len(pieces), high / len(pieces))
        gain = gain * jnp.repeat(jnp.exp(heights), shape[axis_at] // blocks).reshape((-1,) + (1,) * (len(shape) - 1 - axis_at))
    return gain


def noise(key, dims, scale, bound, cuts=(), kind=jnp.bfloat16):
    array = scale * jax.random.normal(key, dims, jnp.float32)
    if cuts:
        array = array * block_scale(key, dims, cuts, -0.22, 0.18)
    return jnp.clip(array, -bound, bound).astype(kind)


def setup_inputs(seed: int = 0) -> dict:
    arg_keys = jax.random.split(jax.random.key(seed), 4)
    return {
        "section_inputs": noise(arg_keys[0], (SECTIONS, MICRO, LAT, NLON, C), 1.0, 6.0, ((0, 4), (3, 8))),
        "weights": noise(arg_keys[1], (SECTIONS, 2, 3, 3, C, C), (9 * C) ** -0.5, 0.125, ((0, 4),)),
        "out_cot": noise(arg_keys[2], (MICRO, LAT, NLON, C), 1.0, 6.0, ((2, 8),)),
    }


def lat_pad(field):
    return jnp.pad(field, ((1, 1), (0, 0), (0, 0)))

def lon_wrap(field):
    return jnp.concatenate([field[:, -1:], field, field[:, :1]], axis=1)

def padded_of(field):
    return lat_pad(lon_wrap(field))

def convolve(padded, kernel):
    row_count = padded.shape[0] - 2
    col_count = padded.shape[1] - 2
    channels = padded.shape[2]
    running = jnp.zeros((row_count * col_count, kernel.shape[3]), jnp.float32)
    for lat_off in range(3):
        for lon_off in range(3):
            window = padded[lat_off:lat_off + row_count, lon_off:lon_off + col_count].reshape(-1, channels)
            running = running + jnp.dot(window, kernel[lat_off, lon_off], preferred_element_type=jnp.float32)
    return running.reshape(row_count, col_count, -1)

def convolve_back(padded, kernel):
    row_count = padded.shape[0] - 2
    col_count = padded.shape[1] - 2
    channels = padded.shape[2]
    running = jnp.zeros((row_count * col_count, kernel.shape[2]), jnp.float32)
    for lat_off in range(3):
        for lon_off in range(3):
            window = padded[2 - lat_off:2 - lat_off + row_count, 2 - lon_off:2 - lon_off + col_count].reshape(-1, channels)
            running = running + lax.dot_general(window, kernel[lat_off, lon_off], (((1,), (1,)), ((), ())), preferred_element_type=jnp.float32)
    return running.reshape(row_count, col_count, -1)

def correlate(padded, grad):
    row_count = grad.shape[0]
    col_count = grad.shape[1]
    channels = padded.shape[2]
    flat_grad = grad.reshape(-1, grad.shape[2])
    outer = []
    for lat_off in range(3):
        inner = []
        for lon_off in range(3):
            window = padded[lat_off:lat_off + row_count, lon_off:lon_off + col_count].reshape(-1, channels)
            inner.append(lax.dot_general(window, flat_grad, (((0,), (0,)), ((), ())), preferred_element_type=jnp.float32))
        outer.append(jnp.stack(inner))
    return jnp.stack(outer)

def silu_slope(preact):
    sig = jax.nn.sigmoid(preact)
    return sig * (1.0 + preact * (1.0 - sig))

def reference(section_inputs, weights, out_cot):
    section_count = section_inputs.shape[0]
    micro_count = section_inputs.shape[1]
    factor = 1.0 / math.sqrt(micro_count * section_inputs.shape[2] * section_inputs.shape[3])
    chan = section_inputs.shape[4]
    grads_one = [jnp.zeros((3, 3, chan, chan), jnp.float32) for _ in range(section_count)]
    grads_two = [jnp.zeros((3, 3, chan, chan), jnp.float32) for _ in range(section_count)]
    act_rows = [[None] * micro_count for _ in range(section_count)]
    for batch_idx in range(micro_count):
        cotangent = out_cot[batch_idx]
        for section_idx in range(section_count - 1, -1, -1):
            padded_in = padded_of(section_inputs[section_idx, batch_idx])
            preact = convolve(padded_in, weights[section_idx, 0])
            hidden = jax.nn.silu(preact).astype(jnp.bfloat16)
            hidden_grad = convolve_back(padded_of(cotangent), weights[section_idx, 1])
            preact_grad = (hidden_grad * silu_slope(preact)).astype(jnp.bfloat16)
            input_grad = (cotangent.astype(jnp.float32) + convolve_back(padded_of(preact_grad), weights[section_idx, 0])).astype(jnp.bfloat16)
            grads_two[section_idx] = grads_two[section_idx] + correlate(padded_of(hidden), cotangent)
            grads_one[section_idx] = grads_one[section_idx] + correlate(padded_in, preact_grad)
            act_rows[section_idx][batch_idx] = input_grad
            cotangent = input_grad
    act_grads = jnp.stack([jnp.stack(row) for row in act_rows])
    weight_grads = jnp.stack([jnp.stack([grads_one[idx], grads_two[idx]]) for idx in range(section_count)]) * factor
    return (act_grads, weight_grads)
```

```python
import functools
import math

import jax
import jax.numpy as jnp
from jax import lax
from jax.experimental import pallas as pl
from jax.experimental.pallas import tpu as pltpu
from jax.sharding import PartitionSpec as P

MESH = pl.DeviceIdType.MESH
F32 = jnp.float32
BF16 = jnp.bfloat16
SPLIT = 2


def remote(src, dst, send_sem, recv_sem, where):
    return pltpu.make_async_remote_copy(
        src_ref=src,
        dst_ref=dst,
        send_sem=send_sem,
        recv_sem=recv_sem,
        device_id=where,
        device_id_type=MESH,
    )


def shift_lat(value, by, lat):
    rows, chans = value.shape
    rolled = pltpu.roll(value, by % rows, 0).reshape(rows // lat, lat, chans)
    row = lax.broadcasted_iota(jnp.int32, rolled.shape, 1)
    edge = 0 if by > 0 else lat - 1
    return jnp.where(row == edge, 0.0, rolled).reshape(rows, chans)


def three_by_three(read, weight, lat, contract):
    total = None
    for a in (1, 0, 2):
        part = None
        for b in range(3):
            term = lax.dot_general(
                read(b), weight(a, b), (((1,), (contract,)), ((), ())), preferred_element_type=F32
            )
            part = term if part is None else part + term
        if a != 1:
            part = shift_lat(part, 1 - a, lat)
        total = part if total is None else total + part
    return total


def kernel(
    dims, x_ref, w_ref, co_ref, act_ref, g_ref,
    xe, ce, slope, de, xt, ht, part, mine, pr, lr, rr, ls, rs,
    x_send, x_recv, co_send, c_send, c_recv, p_send, p_recv,
    l_send, l_recv, r_send, r_recv, f_send, f_recv,
):
    sections, lons, lat, factor = dims
    micro, cells, chans = x_ref.shape
    chunks, _, rows, _ = g_ref.shape
    line = lons // 2
    wide = cells + 2 * lat
    s = lax.axis_index("section")
    l = lax.axis_index("lon")
    k = l // 2
    core = l % 2
    left = lax.rem(l + lons - 1, lons)
    right = lax.rem(l + 1, lons)
    partner = (s, l + 1 - 2 * core)
    has_up = s < sections - 1
    has_down = s > 0

    barrier = pltpu.get_barrier_semaphore()

    def greet(sec, lon):
        pl.semaphore_signal(barrier, inc=1, device_id=(sec, lon), device_id_type=MESH)

    greet(s, left)
    greet(s, right)

    @pl.when(k > 0)
    def _():
        greet(s, l - 2)

    @pl.when(k < line - 1)
    def _():
        greet(s, l + 2)

    @pl.when(has_down)
    def _():
        for lon in (left, l, right):
            greet(s - 1, lon)

    @pl.when(has_up)
    def _():
        for lon in (left, l, right):
            greet(s + 1, lon)

    line_peers = jnp.where(k > 0, 1, 0) + jnp.where(k < line - 1, 1, 0)
    chain_peers = jnp.where(has_down, 3, 0) + jnp.where(has_up, 3, 0)
    pl.semaphore_wait(barrier, 2 + line_peers + chain_peers)

    def edge_right(src, dst, m, sec, send, recv):
        return remote(
            src.at[m, pl.ds(cells - 2 * lat, 2 * lat)], dst.at[m, pl.ds(0, 2 * lat)], send, recv, (sec, right)
        )

    def edge_left(src, dst, m, sec, send, recv):
        return remote(
            src.at[m, pl.ds(0, 2 * lat)],
            dst.at[m, pl.ds(cells + 2 * lat, 2 * lat)],
            send,
            recv,
            (sec, left),
        )

    def x_edges(m):
        return (
            edge_right(x_ref, xe, m, s, x_send.at[m, 0], x_recv.at[m, 0]),
            edge_left(x_ref, xe, m, s, x_send.at[m, 1], x_recv.at[m, 1]),
        )

    def co_edges(m):
        return (
            edge_right(co_ref, ce, m, s, co_send.at[m, 0], c_recv.at[m, 0]),
            edge_left(co_ref, ce, m, s, co_send.at[m, 1], c_recv.at[m, 1]),
        )

    def hops(m):
        return (
            edge_right(act_ref, ce, m, s - 1, c_send.at[m, 0], c_recv.at[m, 0]),
            edge_left(act_ref, ce, m, s - 1, c_send.at[m, 1], c_recv.at[m, 1]),
            remote(
                act_ref.at[m],
                ce.at[m, pl.ds(2 * lat, cells)],
                c_send.at[m, 2],
                c_recv.at[m, 2],
                (s - 1, l),
            ),
        )

    for m in range(micro):
        for copy in x_edges(m):
            copy.start()

    @pl.when(s == sections - 1)
    def _():
        for m in range(micro):
            for copy in co_edges(m):
                copy.start()
            ce[m, pl.ds(2 * lat, cells)] = co_ref[m]

    def lifted(value, dest, m):
        wide_value = value.astype(F32)
        for a in range(3):
            moved = wide_value if a == 1 else shift_lat(wide_value, 1 - a, lat)
            dest[m, a] = jnp.transpose(moved).astype(BF16)

    def forward(m, carry):
        xe[m, pl.ds(2 * lat, cells)] = x_ref[m]
        lifted(x_ref[m], xt, m)
        for copy in x_edges(m):
            copy.wait_recv()
        z = three_by_three(
            lambda b: xe[m, pl.ds(b * lat, wide)], lambda a, b: w_ref[3 * a + b], lat, 0
        )
        sig = jax.nn.sigmoid(z)
        slope[m] = sig * (1.0 + z * (1.0 - sig))
        hidden = (z * sig)[lat : lat + cells].astype(BF16)
        lifted(hidden, ht, m)
        return carry

    lax.fori_loop(0, micro, forward, 0)

    @pl.when(k == 0)
    def _():
        lr[...] = jnp.zeros_like(lr)

    @pl.when(k == line - 1)
    def _():
        rr[...] = jnp.zeros_like(rr)

    def chain(m, carry):
        @pl.when(has_up)
        def _():
            hops(m)[2].wait_recv()

        for copy in co_edges(m):
            copy.wait_recv()
        back = three_by_three(
            lambda b: ce[m, pl.ds(b * lat, wide)], lambda a, b: w_ref[17 - 3 * a - b], lat, 1
        )
        de[m] = (back * slope[m]).astype(BF16)
        down = three_by_three(
            lambda b: de[m, pl.ds(b * lat, cells)], lambda a, b: w_ref[8 - 3 * a - b], lat, 1
        )
        act_ref[m] = (ce[m, pl.ds(2 * lat, cells)].astype(F32) + down).astype(BF16)

        @pl.when(has_down)
        def _():
            for copy in hops(m):
                copy.start()

        return carry

    lax.fori_loop(0, micro, chain, 0)

    def pair(n):
        return remote(
            part.at[n, 1 - core], pr.at[n], p_send.at[n], p_recv.at[n], partner
        )

    def correlate(lifted_ref, grad_ref, base, margin):
        def one(b, carry):
            start = pl.multiple_of((margin + 1 - b) * lat, lat)
            for a in range(3):
                total = None
                for m in range(micro):
                    term = jnp.dot(
                        lifted_ref[m, a], grad_ref[m, pl.ds(start, cells)], preferred_element_type=F32
                    )
                    total = term if total is None else total + term
                tile = (total * factor).astype(BF16)
                lo = a * chans
                while lo < (a + 1) * chans:
                    block, inner = lo // rows, lo % rows
                    hi = min((block + 1) * rows, (a + 1) * chans)
                    part[base + SPLIT * b + block // 2, block % 2, inner : inner + hi - lo] = tile[
                        lo - a * chans : hi - a * chans
                    ]
                    lo = hi
            for q in range(SPLIT):
                pair(base + SPLIT * b + q).start()
            return carry

        lax.fori_loop(0, 3, one, 0)

    correlate(ht, ce, 0, 2)
    correlate(xt, de, 3 * SPLIT, 1)

    def to_right(n):
        return remote(ls.at[n], lr.at[n], l_send.at[n], l_recv.at[n], (s, l + 2))

    def to_left(n):
        return remote(rs.at[n], rr.at[n], r_send.at[n], r_recv.at[n], (s, l - 2))

    def final(n):
        return remote(g_ref.at[n, core], g_ref.at[n, core], f_send.at[n], f_recv.at[n], partner)

    def step(t, carry):
        @pl.when(t < chunks)
        def _():
            pair(t).wait_recv()
            mine[t] = part[t, core].astype(F32) + pr[t].astype(F32)

        i = t - k

        @pl.when((i >= 0) & (i < chunks))
        def _():
            @pl.when(k > 0)
            def _():
                to_right(i).wait_recv()

            @pl.when(k < line - 1)
            def _():
                ls[i] = (mine[i] + lr[i].astype(F32)).astype(BF16)
                to_right(i).start()

        j = t - (line - 1 - k)

        @pl.when((j >= 0) & (j < chunks))
        def _():
            @pl.when(k < line - 1)
            def _():
                to_left(j).wait_recv()

            @pl.when(k > 0)
            def _():
                rs[j] = (mine[j] + rr[j].astype(F32)).astype(BF16)
                to_left(j).start()

        n = t - (line - 1)

        @pl.when(n >= 0)
        def _():
            g_ref[n, core] = (mine[n] + lr[n].astype(F32) + rr[n].astype(F32)).astype(BF16)
            final(n).start()

        return carry

    lax.fori_loop(0, chunks + line - 1, step, 0)

    def settle(n, carry):
        pair(n).wait_send()
        final(n).wait_send()
        remote(
            g_ref.at[n, 1 - core], g_ref.at[n, 1 - core], f_send.at[n], f_recv.at[n], partner
        ).wait_recv()

        @pl.when(k < line - 1)
        def _():
            to_right(n).wait_send()

        @pl.when(k > 0)
        def _():
            to_left(n).wait_send()

        return carry

    lax.fori_loop(0, chunks, settle, 0)

    for m in range(micro):
        for copy in x_edges(m):
            copy.wait_send()

        @pl.when(s == sections - 1)
        def _():
            for copy in co_edges(m):
                copy.wait_send()

        @pl.when(has_down)
        def _():
            for copy in hops(m):
                copy.wait_send()


def local(sections, lons, section_inputs, weights, out_cot):
    _, micro, lat, cols, chans = section_inputs.shape
    factor = 1.0 / math.sqrt(micro * lat * cols * lons)
    cells = lat * cols
    x = section_inputs[0].transpose(0, 2, 1, 3).reshape(micro, cells, chans)
    co = out_cot.transpose(0, 2, 1, 3).reshape(micro, cells, chans)
    w = weights.reshape(18, chans, chans)
    chunks = 6 * SPLIT
    rows = 3 * chans // (2 * SPLIT)
    wide = cells + 2 * lat
    dma = pltpu.SemaphoreType.DMA
    vmem = pl.BlockSpec(memory_space=pltpu.VMEM)
    piece = (chunks, rows, chans)
    act, grads = pl.pallas_call(
        functools.partial(kernel, (sections, lons, lat, factor)),
        out_shape=(
            jax.ShapeDtypeStruct((micro, cells, chans), BF16),
            jax.ShapeDtypeStruct((chunks, 2, rows, chans), BF16),
        ),
        in_specs=[vmem] * 3,
        out_specs=(vmem, vmem),
        scratch_shapes=[
            pltpu.VMEM((micro, cells + 4 * lat, chans), BF16),
            pltpu.VMEM((micro, cells + 4 * lat, chans), BF16),
            pltpu.VMEM((micro, wide, chans), F32),
            pltpu.VMEM((micro, wide, chans), BF16),
            pltpu.VMEM((micro, 3, chans, cells), BF16),
            pltpu.VMEM((micro, 3, chans, cells), BF16),
            pltpu.VMEM((chunks, 2, rows, chans), BF16),
            pltpu.VMEM(piece, F32),
            pltpu.VMEM(piece, BF16),
            pltpu.VMEM(piece, BF16),
            pltpu.VMEM(piece, BF16),
            pltpu.VMEM(piece, BF16),
            pltpu.VMEM(piece, BF16),
            dma((micro, 2)),
            dma((micro, 2)),
            dma((micro, 2)),
            dma((micro, 3)),
            dma((micro, 3)),
        ]
        + [dma((chunks,))] * 8,
        compiler_params=pltpu.CompilerParams(
            collective_id=0, has_side_effects=True, vmem_limit_bytes=40 * 1024 * 1024
        ),
    )(x, w, co)
    act = act.reshape(micro, cols, lat, chans).transpose(0, 2, 1, 3)
    grads = grads.reshape(2, 3, 3, chans, chans)[::-1].transpose(0, 2, 1, 3, 4).astype(F32)
    return act[None], grads[None]


def solution(mesh):
    placed = (
        P("section", None, None, "lon", None),
        P("section", None, None, None, None, None),
        P(None, None, "lon", None),
    )
    return jax.shard_map(
        functools.partial(local, mesh.shape["section"], mesh.shape["lon"]),
        mesh=mesh,
        in_specs=placed,
        out_specs=(
            P("section", None, None, "lon", None),
            P("section", None, None, None, None, None),
        ),
        check_vma=False,
    )
```

```python
import functools
import math

import jax
import jax.numpy as jnp
from jax import lax
from jax.experimental import pallas as pl
from jax.experimental.pallas import tpu as pltpu
from jax.sharding import PartitionSpec as P

MESH = pl.DeviceIdType.MESH
F32 = jnp.float32
BF16 = jnp.bfloat16
SPLIT = 4
SLACK = 3
SHIFT = 4


def remote(src, dst, send_sem, recv_sem, where):
    return pltpu.make_async_remote_copy(
        src_ref=src,
        dst_ref=dst,
        send_sem=send_sem,
        recv_sem=recv_sem,
        device_id=where,
        device_id_type=MESH,
    )


def shift_lat(value, by, lat):
    rows, chans = value.shape
    rolled = pltpu.roll(value, by % rows, 0).reshape(rows // lat, lat, chans)
    row = lax.broadcasted_iota(jnp.int32, rolled.shape, 1)
    edge = 0 if by > 0 else lat - 1
    return jnp.where(row == edge, 0.0, rolled).reshape(rows, chans)


def three_by_three(read, weight, lat, contract):
    total = None
    for a in (1, 0, 2):
        part = None
        for b in range(3):
            term = lax.dot_general(
                read(b), weight(a, b), (((1,), (contract,)), ((), ())), preferred_element_type=F32
            )
            part = term if part is None else part + term
        if a != 1:
            part = shift_lat(part, 1 - a, lat)
        total = part if total is None else total + part
    return total


def kernel(
    dims, x_ref, w_ref, co_ref, act_ref, g_ref,
    xe, ce, slope, de, xt, ht, part, mine, pr, lr, rr, ls, rs, gift, got,
    x_send, x_recv, co_send, c_send, c_recv, p_send, p_recv,
    l_send, l_recv, r_send, r_recv, f_send, f_recv, g_send, g_recv, o_send, o_recv,
):
    sections, lons, lat, factor, shares = dims
    micro, cells, chans = x_ref.shape
    chunks, _, rows, _ = g_ref.shape
    line = lons // 2
    wide = cells + 2 * lat
    s = lax.axis_index("section")
    l = lax.axis_index("lon")
    k = l // 2
    core = l % 2
    left = lax.rem(l + lons - 1, lons)
    right = lax.rem(l + 1, lons)
    partner = (s, l + 1 - 2 * core)
    has_up = s < sections - 1
    has_down = s > 0
    mirror = (sections - 1 - s, l)
    helps = s > sections - 1 - s
    helped = s < sections - 1 - s
    share = 0
    for i, amount in enumerate(shares):
        share = share + jnp.where(s == i, amount, 0)

    barrier = pltpu.get_barrier_semaphore()

    def greet(sec, lon):
        pl.semaphore_signal(barrier, inc=1, device_id=(sec, lon), device_id_type=MESH)

    greet(s, left)
    greet(s, right)

    @pl.when(k > 0)
    def _():
        greet(s, l - 2)

    @pl.when(k < line - 1)
    def _():
        greet(s, l + 2)

    @pl.when(has_down)
    def _():
        for lon in (left, l, right):
            greet(s - 1, lon)

    @pl.when(has_up)
    def _():
        for lon in (left, l, right):
            greet(s + 1, lon)

    @pl.when(helps | helped)
    def _():
        greet(*mirror)

    mirror_peers = jnp.where(helps, 1, 0) + jnp.where(helped, 1, 0)
    line_peers = jnp.where(k > 0, 1, 0) + jnp.where(k < line - 1, 1, 0)
    chain_peers = jnp.where(has_down, 3, 0) + jnp.where(has_up, 3, 0)
    pl.semaphore_wait(barrier, 2 + line_peers + chain_peers + mirror_peers)

    def edge_right(src, dst, m, sec, send, recv):
        return remote(
            src.at[m, pl.ds(cells - 2 * lat, 2 * lat)], dst.at[m, pl.ds(0, 2 * lat)], send, recv, (sec, right)
        )

    def edge_left(src, dst, m, sec, send, recv):
        return remote(
            src.at[m, pl.ds(0, 2 * lat)],
            dst.at[m, pl.ds(cells + 2 * lat, 2 * lat)],
            send,
            recv,
            (sec, left),
        )

    def x_edges(m):
        return (
            edge_right(x_ref, xe, m, s, x_send.at[m, 0], x_recv.at[m, 0]),
            edge_left(x_ref, xe, m, s, x_send.at[m, 1], x_recv.at[m, 1]),
        )

    def co_edges(m):
        return (
            edge_right(co_ref, ce, m, s, co_send.at[m, 0], c_recv.at[m, 0]),
            edge_left(co_ref, ce, m, s, co_send.at[m, 1], c_recv.at[m, 1]),
        )

    def hops(m):
        return (
            edge_right(act_ref, ce, m, s - 1, c_send.at[m, 0], c_recv.at[m, 0]),
            edge_left(act_ref, ce, m, s - 1, c_send.at[m, 1], c_recv.at[m, 1]),
            remote(
                act_ref.at[m],
                ce.at[m, pl.ds(2 * lat, cells)],
                c_send.at[m, 2],
                c_recv.at[m, 2],
                (s - 1, l),
            ),
        )

    for m in range(micro):
        for copy in x_edges(m):
            copy.start()

    @pl.when(s == sections - 1)
    def _():
        for m in range(micro):
            for copy in co_edges(m):
                copy.start()
            ce[m, pl.ds(2 * lat, cells)] = co_ref[m]

    def lifted(value, dest, m):
        wide_value = value.astype(F32)
        for a in range(3):
            moved = wide_value if a == 1 else shift_lat(wide_value, 1 - a, lat)
            dest[m, a] = jnp.transpose(moved).astype(BF16)

    def section(m, carry):
        xe[m, pl.ds(2 * lat, cells)] = x_ref[m]
        lifted(x_ref[m], xt, m)
        for copy in x_edges(m):
            copy.wait_recv()
        z = three_by_three(
            lambda b: xe[m, pl.ds(b * lat, wide)], lambda a, b: w_ref[3 * a + b], lat, 0
        )
        sig = jax.nn.sigmoid(z)
        slope[m] = sig * (1.0 + z * (1.0 - sig))
        hidden = (z * sig)[lat : lat + cells].astype(BF16)
        lifted(hidden, ht, m)

        @pl.when(has_up)
        def _():
            hops(m)[2].wait_recv()

        for copy in co_edges(m):
            copy.wait_recv()
        back = three_by_three(
            lambda b: ce[m, pl.ds(b * lat, wide)], lambda a, b: w_ref[17 - 3 * a - b], lat, 1
        )
        de[m] = (back * slope[m]).astype(BF16)
        down = three_by_three(
            lambda b: de[m, pl.ds(b * lat, cells)], lambda a, b: w_ref[8 - 3 * a - b], lat, 1
        )
        act_ref[m] = (ce[m, pl.ds(2 * lat, cells)].astype(F32) + down).astype(BF16)

        @pl.when(has_down)
        def _():
            for copy in hops(m):
                copy.start()

        return carry

    lax.fori_loop(0, micro, section, 0)

    @pl.when(k == 0)
    def _():
        lr[...] = jnp.zeros_like(lr)

    @pl.when(k == line - 1)
    def _():
        rr[...] = jnp.zeros_like(rr)

    def pair(n):
        return remote(
            part.at[n, 1 - core], pr.at[n], p_send.at[n], p_recv.at[n], partner
        )

    def correlate(lifted_ref, grad_ref, base, margin):
        def one(b, carry):
            start = pl.multiple_of((margin + 1 - b) * lat, lat)
            for a in range(3):
                total = None
                for m in range(micro):
                    term = jnp.dot(
                        lifted_ref[m, a], grad_ref[m, pl.ds(start, cells)], preferred_element_type=F32
                    )
                    total = term if total is None else total + term
                tile = (total * factor).astype(BF16)
                lo = a * chans
                while lo < (a + 1) * chans:
                    block, inner = lo // rows, lo % rows
                    hi = min((block + 1) * rows, (a + 1) * chans)
                    part[base + SPLIT * b + block // 2, block % 2, inner : inner + hi - lo] = tile[
                        lo - a * chans : hi - a * chans
                    ]
                    lo = hi
            for q in range(SPLIT):
                pair(base + SPLIT * b + q).start()
            return carry

        lax.fori_loop(0, 3, one, 0)

    correlate(ht, ce, 0, 2)
    correlate(xt, de, 3 * SPLIT, 1)

    def to_right(n):
        return remote(ls.at[n], lr.at[n], l_send.at[n], l_recv.at[n], (s, l + 2))

    def to_left(n):
        return remote(rs.at[n], rr.at[n], r_send.at[n], r_recv.at[n], (s, l - 2))

    def final(n):
        return remote(g_ref.at[n, core], g_ref.at[n, core], f_send.at[n], f_recv.at[n], partner)

    def to_helper(i):
        return remote(gift.at[i], got.at[i], g_send.at[i], g_recv.at[i], mirror)

    def to_owner(i):
        dest = g_ref.at[chunks - share + i, core]
        return remote(gift.at[i], dest, o_send.at[i], o_recv.at[i], mirror)

    length = chunks + jnp.where(helps, share, 0) - jnp.where(helped, share, 0)

    def step(t, carry):
        @pl.when((t < length) & (t < chunks))
        def _():
            pair(t).wait_recv()
            mine[t] = part[t, core].astype(F32) + pr[t].astype(F32)

        @pl.when(helped & (t < share))
        def _():
            at = chunks - share + t
            pair(at).wait_recv()
            gift[t] = (part[at, core].astype(F32) + pr[at].astype(F32)).astype(BF16)
            to_helper(t).start()

        @pl.when(helps & (t >= chunks) & (t < length))
        def _():
            to_helper(t - chunks).wait_recv()
            mine[t] = got[t - chunks].astype(F32)

        i = t - SLACK * k

        @pl.when((i >= 0) & (i < length))
        def _():
            @pl.when(k > 0)
            def _():
                to_right(i).wait_recv()

            @pl.when(k < line - 1)
            def _():
                ls[i] = (mine[i] + lr[i].astype(F32)).astype(BF16)
                to_right(i).start()

        j = t - SLACK * (line - 1 - k)

        @pl.when((j >= 0) & (j < length))
        def _():
            @pl.when(k < line - 1)
            def _():
                to_left(j).wait_recv()

            @pl.when(k > 0)
            def _():
                rs[j] = (mine[j] + rr[j].astype(F32)).astype(BF16)
                to_left(j).start()

        n = t - SLACK * (line - 1)

        @pl.when((n >= 0) & (n < chunks))
        def _():
            g_ref[n, core] = (mine[n] + lr[n].astype(F32) + rr[n].astype(F32)).astype(BF16)
            final(n).start()

        @pl.when(n >= chunks)
        def _():
            gift[n - chunks] = (mine[n] + lr[n].astype(F32) + rr[n].astype(F32)).astype(BF16)
            to_owner(n - chunks).start()

        return carry

    lax.fori_loop(0, length + SLACK * (line - 1), step, 0)

    def finish(i, carry):
        @pl.when(helped)
        def _():
            to_owner(i).wait_recv()
            final(chunks - share + i).start()
            to_helper(i).wait_send()

        @pl.when(helps)
        def _():
            to_owner(i).wait_send()

        return carry

    lax.fori_loop(0, share, finish, 0)

    def settle(n, carry):
        pair(n).wait_send()
        final(n).wait_send()
        remote(
            g_ref.at[n, 1 - core], g_ref.at[n, 1 - core], f_send.at[n], f_recv.at[n], partner
        ).wait_recv()

        return carry

    lax.fori_loop(0, chunks, settle, 0)

    def settle_line(n, carry):
        @pl.when(k < line - 1)
        def _():
            to_right(n).wait_send()

        @pl.when(k > 0)
        def _():
            to_left(n).wait_send()

        return carry

    lax.fori_loop(0, length, settle_line, 0)

    for m in range(micro):
        for copy in x_edges(m):
            copy.wait_send()

        @pl.when(s == sections - 1)
        def _():
            for copy in co_edges(m):
                copy.wait_send()

        @pl.when(has_down)
        def _():
            for copy in hops(m):
                copy.wait_send()


def local(sections, lons, section_inputs, weights, out_cot):
    _, micro, lat, cols, chans = section_inputs.shape
    factor = 1.0 / math.sqrt(micro * lat * cols * lons)
    cells = lat * cols
    x = section_inputs[0].transpose(0, 2, 1, 3).reshape(micro, cells, chans)
    co = out_cot.transpose(0, 2, 1, 3).reshape(micro, cells, chans)
    w = weights.reshape(18, chans, chans)
    chunks = 6 * SPLIT
    rows = 3 * chans // (2 * SPLIT)
    wide = cells + 2 * lat
    dma = pltpu.SemaphoreType.DMA
    vmem = pl.BlockSpec(memory_space=pltpu.VMEM)
    piece = (chunks, rows, chans)
    gaps = [abs(sections - 1 - 2 * i) for i in range(sections)]
    shares = [min(chunks // 2, SHIFT * gap) for gap in gaps]
    extra = max(max(shares), 1)
    longer = (chunks + extra, rows, chans)
    act, grads = pl.pallas_call(
        functools.partial(kernel, (sections, lons, lat, factor, shares)),
        out_shape=(
            jax.ShapeDtypeStruct((micro, cells, chans), BF16),
            jax.ShapeDtypeStruct((chunks, 2, rows, chans), BF16),
        ),
        in_specs=[vmem] * 3,
        out_specs=(vmem, vmem),
        scratch_shapes=[
            pltpu.VMEM((micro, cells + 4 * lat, chans), BF16),
            pltpu.VMEM((micro, cells + 4 * lat, chans), BF16),
            pltpu.VMEM((micro, wide, chans), F32),
            pltpu.VMEM((micro, wide, chans), BF16),
            pltpu.VMEM((micro, 3, chans, cells), BF16),
            pltpu.VMEM((micro, 3, chans, cells), BF16),
            pltpu.VMEM((chunks, 2, rows, chans), BF16),
            pltpu.VMEM(longer, F32),
            pltpu.VMEM(piece, BF16),
            pltpu.VMEM(longer, BF16),
            pltpu.VMEM(longer, BF16),
            pltpu.VMEM(longer, BF16),
            pltpu.VMEM(longer, BF16),
            pltpu.VMEM((extra, rows, chans), BF16),
            pltpu.VMEM((extra, rows, chans), BF16),
            dma((micro, 2)),
            dma((micro, 2)),
            dma((micro, 2)),
            dma((micro, 3)),
            dma((micro, 3)),
        ]
        + [dma((chunks,))] * 2
        + [dma((chunks + extra,))] * 4
        + [dma((chunks,))] * 2
        + [dma((extra,))] * 4,
        compiler_params=pltpu.CompilerParams(
            collective_id=0, has_side_effects=True, vmem_limit_bytes=40 * 1024 * 1024
        ),
    )(x, w, co)
    act = act.reshape(micro, cols, lat, chans).transpose(0, 2, 1, 3)
    grads = grads.reshape(2, 3, 3, chans, chans)[::-1].transpose(0, 2, 1, 3, 4).astype(F32)
    return act[None], grads[None]


def solution(mesh):
    placed = (
        P("section", None, None, "lon", None),
        P("section", None, None, None, None, None),
        P(None, None, "lon", None),
    )
    return jax.shard_map(
        functools.partial(local, mesh.shape["section"], mesh.shape["lon"]),
        mesh=mesh,
        in_specs=placed,
        out_specs=(
            P("section", None, None, "lon", None),
            P("section", None, None, None, None, None),
        ),
        check_vma=False,
    )
```

```python
import functools
import math

import jax
import jax.numpy as jnp
from jax import lax
from jax.experimental import pallas as pl
from jax.experimental.pallas import tpu as pltpu
from jax.sharding import PartitionSpec as P

MESH = pl.DeviceIdType.MESH
F32 = jnp.float32
BF16 = jnp.bfloat16
SPLIT = 4
SLACK = 3
SHIFT = 3


def remote(src, dst, send_sem, recv_sem, where):
    return pltpu.make_async_remote_copy(
        src_ref=src,
        dst_ref=dst,
        send_sem=send_sem,
        recv_sem=recv_sem,
        device_id=where,
        device_id_type=MESH,
    )


def shift_lat(value, by, lat):
    rows, chans = value.shape
    rolled = pltpu.roll(value, by % rows, 0).reshape(rows // lat, lat, chans)
    row = lax.broadcasted_iota(jnp.int32, rolled.shape, 1)
    edge = 0 if by > 0 else lat - 1
    return jnp.where(row == edge, 0.0, rolled).reshape(rows, chans)


def three_by_three(read, weight, lat, contract):
    total = None
    for a in (1, 0, 2):
        part = None
        for b in range(3):
            term = lax.dot_general(
                read(b), weight(a, b), (((1,), (contract,)), ((), ())), preferred_element_type=F32
            )
            part = term if part is None else part + term
        if a != 1:
            part = shift_lat(part, 1 - a, lat)
        total = part if total is None else total + part
    return total


def kernel(
    dims, x_ref, w_ref, co_ref, act_ref, g_ref,
    xe, ce, slope, de, xt, ht, part, mine, pr, lr, rr, ls, rs, gift, got, held,
    x_send, x_recv, co_send, c_send, c_recv, p_send, p_recv,
    l_send, l_recv, r_send, r_recv, f_send, f_recv, g_send, g_recv, o_send, o_recv,
):
    sections, lons, lat, factor, shares = dims
    micro, cells, chans = x_ref.shape
    chunks, _, rows, _ = g_ref.shape
    line = lons // 2
    wide = cells + 2 * lat
    s = lax.axis_index("section")
    l = lax.axis_index("lon")
    k = l // 2
    core = l % 2
    left = lax.rem(l + lons - 1, lons)
    right = lax.rem(l + 1, lons)
    partner = (s, l + 1 - 2 * core)
    has_up = s < sections - 1
    has_down = s > 0
    mirror = (sections - 1 - s, l)
    helps = s > sections - 1 - s
    helped = s < sections - 1 - s
    share = 0
    for i, amount in enumerate(shares):
        share = share + jnp.where(s == i, amount, 0)

    barrier = pltpu.get_barrier_semaphore()

    def greet(sec, lon):
        pl.semaphore_signal(barrier, inc=1, device_id=(sec, lon), device_id_type=MESH)

    greet(s, left)
    greet(s, right)

    @pl.when(k > 0)
    def _():
        greet(s, l - 2)

    @pl.when(k < line - 1)
    def _():
        greet(s, l + 2)

    @pl.when(has_down)
    def _():
        for lon in (left, l, right):
            greet(s - 1, lon)

    @pl.when(has_up)
    def _():
        for lon in (left, l, right):
            greet(s + 1, lon)

    @pl.when(helps | helped)
    def _():
        greet(*mirror)

    mirror_peers = jnp.where(helps, 1, 0) + jnp.where(helped, 1, 0)
    line_peers = jnp.where(k > 0, 1, 0) + jnp.where(k < line - 1, 1, 0)
    chain_peers = jnp.where(has_down, 3, 0) + jnp.where(has_up, 3, 0)
    pl.semaphore_wait(barrier, 2 + line_peers + chain_peers + mirror_peers)

    def edge_right(src, dst, m, sec, send, recv):
        return remote(
            src.at[m, pl.ds(cells - 2 * lat, 2 * lat)], dst.at[m, pl.ds(0, 2 * lat)], send, recv, (sec, right)
        )

    def edge_left(src, dst, m, sec, send, recv):
        return remote(
            src.at[m, pl.ds(0, 2 * lat)],
            dst.at[m, pl.ds(cells + 2 * lat, 2 * lat)],
            send,
            recv,
            (sec, left),
        )

    def x_edges(m):
        return (
            edge_right(x_ref, xe, m, s, x_send.at[m, 0], x_recv.at[m, 0]),
            edge_left(x_ref, xe, m, s, x_send.at[m, 1], x_recv.at[m, 1]),
        )

    def co_edges(m):
        return (
            edge_right(co_ref, ce, m, s, co_send.at[m, 0], c_recv.at[m, 0]),
            edge_left(co_ref, ce, m, s, co_send.at[m, 1], c_recv.at[m, 1]),
        )

    def hops(m):
        return (
            edge_right(act_ref, ce, m, s - 1, c_send.at[m, 0], c_recv.at[m, 0]),
            edge_left(act_ref, ce, m, s - 1, c_send.at[m, 1], c_recv.at[m, 1]),
            remote(
                act_ref.at[m],
                ce.at[m, pl.ds(2 * lat, cells)],
                c_send.at[m, 2],
                c_recv.at[m, 2],
                (s - 1, l),
            ),
        )

    for m in range(micro):
        for copy in x_edges(m):
            copy.start()

    @pl.when(s == sections - 1)
    def _():
        for m in range(micro):
            for copy in co_edges(m):
                copy.start()
            ce[m, pl.ds(2 * lat, cells)] = co_ref[m]

    def lifted(value, dest, m):
        wide_value = value.astype(F32)
        for a in range(3):
            moved = wide_value if a == 1 else shift_lat(wide_value, 1 - a, lat)
            dest[m, a] = jnp.transpose(moved).astype(BF16)

    def section(m, carry):
        xe[m, pl.ds(2 * lat, cells)] = x_ref[m]
        for copy in x_edges(m):
            copy.wait_recv()
        z = three_by_three(
            lambda b: xe[m, pl.ds(b * lat, wide)], lambda a, b: w_ref[3 * a + b], lat, 0
        )
        sig = jax.nn.sigmoid(z)
        slope[m] = sig * (1.0 + z * (1.0 - sig))
        held[m] = (z * sig)[lat : lat + cells].astype(BF16)

        def lift():
            lifted(xe[m, pl.ds(2 * lat, cells)], xt, m)
            lifted(held[m], ht, m)

        pl.when(has_up)(lift)

        @pl.when(has_up)
        def _():
            hops(m)[2].wait_recv()

        for copy in co_edges(m):
            copy.wait_recv()
        back = three_by_three(
            lambda b: ce[m, pl.ds(b * lat, wide)], lambda a, b: w_ref[17 - 3 * a - b], lat, 1
        )
        de[m] = (back * slope[m]).astype(BF16)
        down = three_by_three(
            lambda b: de[m, pl.ds(b * lat, cells)], lambda a, b: w_ref[8 - 3 * a - b], lat, 1
        )
        act_ref[m] = (ce[m, pl.ds(2 * lat, cells)].astype(F32) + down).astype(BF16)

        @pl.when(has_down)
        def _():
            for copy in hops(m):
                copy.start()

        pl.when(s == sections - 1)(lift)

        return carry

    lax.fori_loop(0, micro, section, 0)

    @pl.when(k == 0)
    def _():
        lr[...] = jnp.zeros_like(lr)

    @pl.when(k == line - 1)
    def _():
        rr[...] = jnp.zeros_like(rr)

    def pair(n):
        return remote(
            part.at[n, 1 - core], pr.at[n], p_send.at[n], p_recv.at[n], partner
        )

    def correlate(lifted_ref, grad_ref, base, margin):
        def one(b, carry):
            start = pl.multiple_of((margin + 1 - b) * lat, lat)
            for a in range(3):
                total = None
                for m in range(micro):
                    term = jnp.dot(
                        lifted_ref[m, a], grad_ref[m, pl.ds(start, cells)], preferred_element_type=F32
                    )
                    total = term if total is None else total + term
                tile = (total * factor).astype(BF16)
                lo = a * chans
                while lo < (a + 1) * chans:
                    block, inner = lo // rows, lo % rows
                    hi = min((block + 1) * rows, (a + 1) * chans)
                    part[base + SPLIT * b + block // 2, block % 2, inner : inner + hi - lo] = tile[
                        lo - a * chans : hi - a * chans
                    ]
                    lo = hi
            for q in range(SPLIT):
                pair(base + SPLIT * b + q).start()
            return carry

        lax.fori_loop(0, 3, one, 0)

    correlate(ht, ce, 0, 2)
    correlate(xt, de, 3 * SPLIT, 1)

    def to_right(n):
        return remote(ls.at[n], lr.at[n], l_send.at[n], l_recv.at[n], (s, l + 2))

    def to_left(n):
        return remote(rs.at[n], rr.at[n], r_send.at[n], r_recv.at[n], (s, l - 2))

    def final(n):
        return remote(g_ref.at[n, core], g_ref.at[n, core], f_send.at[n], f_recv.at[n], partner)

    def to_helper(i):
        return remote(gift.at[i], got.at[i], g_send.at[i], g_recv.at[i], mirror)

    def to_owner(i):
        dest = g_ref.at[chunks - share + i, core]
        return remote(gift.at[i], dest, o_send.at[i], o_recv.at[i], mirror)

    length = chunks + jnp.where(helps, share, 0) - jnp.where(helped, share, 0)

    def step(t, carry):
        @pl.when((t < length) & (t < chunks))
        def _():
            pair(t).wait_recv()
            mine[t] = part[t, core].astype(F32) + pr[t].astype(F32)

        @pl.when(helped & (t < share))
        def _():
            at = chunks - share + t
            pair(at).wait_recv()
            gift[t] = (part[at, core].astype(F32) + pr[at].astype(F32)).astype(BF16)
            to_helper(t).start()

        @pl.when(helps & (t >= chunks) & (t < length))
        def _():
            to_helper(t - chunks).wait_recv()
            mine[t] = got[t - chunks].astype(F32)

        i = t - SLACK * k

        @pl.when((i >= 0) & (i < length))
        def _():
            @pl.when(k > 0)
            def _():
                to_right(i).wait_recv()

            @pl.when(k < line - 1)
            def _():
                ls[i] = (mine[i] + lr[i].astype(F32)).astype(BF16)
                to_right(i).start()

        j = t - SLACK * (line - 1 - k)

        @pl.when((j >= 0) & (j < length))
        def _():
            @pl.when(k < line - 1)
            def _():
                to_left(j).wait_recv()

            @pl.when(k > 0)
            def _():
                rs[j] = (mine[j] + rr[j].astype(F32)).astype(BF16)
                to_left(j).start()

        n = t - SLACK * (line - 1)

        @pl.when((n >= 0) & (n < chunks))
        def _():
            g_ref[n, core] = (mine[n] + lr[n].astype(F32) + rr[n].astype(F32)).astype(BF16)
            final(n).start()

        @pl.when(n >= chunks)
        def _():
            gift[n - chunks] = (mine[n] + lr[n].astype(F32) + rr[n].astype(F32)).astype(BF16)
            to_owner(n - chunks).start()

        return carry

    lax.fori_loop(0, length + SLACK * (line - 1), step, 0)

    def finish(i, carry):
        @pl.when(helped)
        def _():
            to_owner(i).wait_recv()
            final(chunks - share + i).start()
            to_helper(i).wait_send()

        @pl.when(helps)
        def _():
            to_owner(i).wait_send()

        return carry

    lax.fori_loop(0, share, finish, 0)

    def settle(n, carry):
        pair(n).wait_send()
        final(n).wait_send()
        remote(
            g_ref.at[n, 1 - core], g_ref.at[n, 1 - core], f_send.at[n], f_recv.at[n], partner
        ).wait_recv()

        return carry

    lax.fori_loop(0, chunks, settle, 0)

    def settle_line(n, carry):
        @pl.when(k < line - 1)
        def _():
            to_right(n).wait_send()

        @pl.when(k > 0)
        def _():
            to_left(n).wait_send()

        return carry

    lax.fori_loop(0, length, settle_line, 0)

    for m in range(micro):
        for copy in x_edges(m):
            copy.wait_send()

        @pl.when(s == sections - 1)
        def _():
            for copy in co_edges(m):
                copy.wait_send()

        @pl.when(has_down)
        def _():
            for copy in hops(m):
                copy.wait_send()


def local(sections, lons, section_inputs, weights, out_cot):
    _, micro, lat, cols, chans = section_inputs.shape
    factor = 1.0 / math.sqrt(micro * lat * cols * lons)
    cells = lat * cols
    x = section_inputs[0].transpose(0, 2, 1, 3).reshape(micro, cells, chans)
    co = out_cot.transpose(0, 2, 1, 3).reshape(micro, cells, chans)
    w = weights.reshape(18, chans, chans)
    chunks = 6 * SPLIT
    rows = 3 * chans // (2 * SPLIT)
    wide = cells + 2 * lat
    dma = pltpu.SemaphoreType.DMA
    vmem = pl.BlockSpec(memory_space=pltpu.VMEM)
    piece = (chunks, rows, chans)
    gaps = [abs(sections - 1 - 2 * i) for i in range(sections)]
    shares = [min(chunks // 2, SHIFT * gap) for gap in gaps]
    extra = max(max(shares), 1)
    longer = (chunks + extra, rows, chans)
    act, grads = pl.pallas_call(
        functools.partial(kernel, (sections, lons, lat, factor, shares)),
        out_shape=(
            jax.ShapeDtypeStruct((micro, cells, chans), BF16),
            jax.ShapeDtypeStruct((chunks, 2, rows, chans), BF16),
        ),
        in_specs=[vmem] * 3,
        out_specs=(vmem, vmem),
        scratch_shapes=[
            pltpu.VMEM((micro, cells + 4 * lat, chans), BF16),
            pltpu.VMEM((micro, cells + 4 * lat, chans), BF16),
            pltpu.VMEM((micro, wide, chans), F32),
            pltpu.VMEM((micro, wide, chans), BF16),
            pltpu.VMEM((micro, 3, chans, cells), BF16),
            pltpu.VMEM((micro, 3, chans, cells), BF16),
            pltpu.VMEM((chunks, 2, rows, chans), BF16),
            pltpu.VMEM(longer, F32),
            pltpu.VMEM(piece, BF16),
            pltpu.VMEM(longer, BF16),
            pltpu.VMEM(longer, BF16),
            pltpu.VMEM(longer, BF16),
            pltpu.VMEM(longer, BF16),
            pltpu.VMEM((extra, rows, chans), BF16),
            pltpu.VMEM((extra, rows, chans), BF16),
            pltpu.VMEM((micro, cells, chans), BF16),
            dma((micro, 2)),
            dma((micro, 2)),
            dma((micro, 2)),
            dma((micro, 3)),
            dma((micro, 3)),
        ]
        + [dma((chunks,))] * 2
        + [dma((chunks + extra,))] * 4
        + [dma((chunks,))] * 2
        + [dma((extra,))] * 4,
        compiler_params=pltpu.CompilerParams(
            collective_id=0, has_side_effects=True, vmem_limit_bytes=40 * 1024 * 1024
        ),
    )(x, w, co)
    act = act.reshape(micro, cols, lat, chans).transpose(0, 2, 1, 3)
    grads = grads.reshape(2, 3, 3, chans, chans)[::-1].transpose(0, 2, 1, 3, 4).astype(F32)
    return act[None], grads[None]


def solution(mesh):
    placed = (
        P("section", None, None, "lon", None),
        P("section", None, None, None, None, None),
        P(None, None, "lon", None),
    )
    return jax.shard_map(
        functools.partial(local, mesh.shape["section"], mesh.shape["lon"]),
        mesh=mesh,
        in_specs=placed,
        out_specs=(
            P("section", None, None, "lon", None),
            P("section", None, None, None, None, None),
        ),
        check_vma=False,
    )
```
